32 devices in a mesh: dp: 4 (over y, core), expert: 8 (over z, x).
Axes of the slice: x: 2, y: 2, z: 4, core: 2. Of those that a mesh axis runs over, the one named last changes fastest.
Arguments:
- hidden_in: bfloat16 [2048, 7168], P(('dp', 'expert')), may hold values from -6 to 6
- norm_gain: float32 [7168], replicated, may hold values from 0.25 to 4
- route_logits: float32 [2048, 8], P(('dp', 'expert')), may hold values from -6 to 6
- expert_ids: int32 [2048, 8], P(('dp', 'expert')), may hold values from 0 to 255, as said below
- w_gate: bfloat16 [8, 7168, 2048], P('dp', None, 'expert'), may hold values from -0.0625 to 0.0625
- w_up: bfloat16 [8, 7168, 2048], P('dp', None, 'expert'), may hold values from -0.0625 to 0.0625
- w_down: bfloat16 [8, 2048, 7168], P('dp', 'expert'), may hold values from -0.125 to 0.125
- w_latent: bfloat16 [7168, 576], P(('dp', 'expert')), may hold values from -0.0625 to 0.0625
- kv_gain: float32 [512], replicated, may hold values from 0.25 to 4
- queries: bfloat16 [2048, 36864], P(('dp', 'expert')), may hold values from -240 to 240
- page_pool: bfloat16 [4096, 9216], P(('dp', 'expert')), may hold values from -6 to 6
- page_table: int32 [2048, 6], P(('dp', 'expert')), may hold values from 0 to 143
- kv_lengths: int32 [2048], P(('dp', 'expert')), may hold values from 1 to 96, 98304 in all
- migration: int32 [4, 8, 4, 4], P('dp', 'expert'), may hold values from 0 to 127
Outputs:
- hidden_out: bfloat16 [2048, 7168], P(('dp', 'expert'))
- attended: bfloat16 [2048, 32768], P(('dp', 'expert'))
The draws below stay inside these ranges and needn't reach their ends.
Inputs may be any that keep to these rules, and one draw needn't show every extreme that they name: `expert_ids`: each row names 8 different experts, at most one of them below 8. The rows of one device name one window expert at most 4 times; in every draw one window expert is named exactly 4 times by the rows of every device.
All inputs are finite; a program needn't handle non-finite values. No bound on the sum of `kv_lengths` on one device may be relied on, other than what follows from the above.
Results may differ from the reference program's by a relative error of at most 0.038.
Values may be sent and summed in bfloat16 or wider, within the bound.
A program may use at most 192 MiB of HBM per device.

```python
import math
import jax
import jax.numpy as jnp
import numpy as np
from jax import lax

D = 7168
MOE_FF = 2048
NEXP = 256
TOP = 8
HEADS = 64
LATENT = 512
ROPE = 64
PAGE = 16
MAXP = 6
CAP = 4
MCAP = 4
TOK_DEV = 64
POOL_DEV = 128
WIN = 8
FF_DEV = 256
KVW = 576
ROWS = 2048
POOLS = 4096
EXTENDED = 144
N_DP = 4
N_EXPERT = 8


def draw_expert_ids(key, part):
    blocks = ROWS // TOK_DEV
    stride = TOK_DEV // CAP
    keys = jax.random.split(key, 6)
    full_one = jax.random.randint(keys[0], (), 0, WIN)
    counts = jax.random.randint(keys[1], (blocks, WIN), 1, CAP + 1)
    counts = jnp.where(jnp.arange(WIN)[None, :] == full_one, CAP, counts)
    orders = jax.vmap(lambda k: jax.random.permutation(k, WIN))(jax.random.split(keys[2], blocks))
    shifts = jax.random.randint(keys[3], (blocks, 1), 0, TOK_DEV)
    offsets = (jnp.arange(TOK_DEV)[None, :] - shifts) % TOK_DEV
    residue = offsets % stride
    level = offsets // stride
    inside = residue < WIN
    expert_of = jnp.take_along_axis(orders, jnp.minimum(residue, WIN - 1), axis=1)
    count_of = jnp.take_along_axis(counts, expert_of, axis=1)
    inside = inside & (level < count_of)
    position = jax.random.randint(keys[4], (blocks, TOK_DEV), 0, TOP)
    base = jax.random.randint(keys[5], (blocks, TOK_DEV), 0, NEXP - WIN)
    outside = WIN + (base[:, :, None] + jnp.arange(TOP)[None, None, :]) % (NEXP - WIN)
    place = inside[:, :, None] & (jnp.arange(TOP)[None, None, :] == position[:, :, None])
    ids = jnp.where(place, expert_of[:, :, None], outside)
    return ids.reshape(ROWS, TOP).astype(jnp.int32)


def draw_queries(key, part):
    values = jnp.clip(jax.random.normal(key, (ROWS, HEADS * KVW), jnp.float32), -6.0, 6.0)
    return values.astype(jnp.bfloat16)


def plant(values, stream_key, smallest, largest):
    longest = values.shape.index(max(values.shape))
    spots = []
    for shift in (0, 1):
        where = [jax.random.randint(jax.random.fold_in(stream_key, axis), (), 0, length) for axis, length in enumerate(values.shape)]
        where[longest] = (where[longest] + shift) % values.shape[longest]
        spots.append(tuple(where))
    return values.at[spots[0]].set(smallest).at[spots[1]].set(largest)


def shard_levels(key, extent, cuts, low, high):
    level, own = 1.0, jax.random.fold_in(key, 6)
    for dim, blocks in cuts:
        draws = jnp.exp(jax.random.uniform(jax.random.fold_in(own, dim), (blocks,), jnp.float32, low / len(cuts), high / len(cuts)))
        level = level * jnp.repeat(draws, extent[dim] // blocks).reshape([-1 if axis == dim else 1 for axis in range(len(extent))])
    return level


def profile(count, total, limit, skew):
    portions = [(1 << 20) // math.isqrt(rank ** skew) + 1 for rank in range(2, count + 1)]
    rest, given = total - limit - (count - 1), [1] * (count - 1)
    while rest > 0:
        candidates = [i for i in range(count - 1) if given[i] < limit]
        whole, budget = sum([portions[i] for i in candidates]), rest
        for i in candidates:
            addition = min(limit - given[i], max(1, budget * portions[i] // whole), rest)
            given[i] = given[i] + addition
            rest = rest - addition
    return np.array([limit] + given)


def uneven(own_key, amount, total, bound, slope):
    if amount == 2:
        one = jax.random.randint(own_key, (), max(1, total - bound), min(bound, total - 1) + 1)
        return jnp.stack([one, total - one])
    lengths = jnp.asarray(profile(amount, total, bound, slope), jnp.int32)
    couples = (amount - 1) // 2
    giver, taker = lengths[1:1 + 2 * couples:2], lengths[2:2 + 2 * couples:2]
    margin = jnp.minimum(giver - 1, bound - taker)
    shifted = jax.random.randint(jax.random.fold_in(own_key, 1), (couples,), 0, 1 << 20) % (margin + 1)
    lengths = lengths.at[1:1 + 2 * couples:2].set(giver - shifted).at[2:2 + 2 * couples:2].set(taker + shifted)
    return lengths[jax.random.permutation(jax.random.fold_in(own_key, 2), amount)]


def gaussian(own_key, shape, deviation, reach, pieces=(), kind=jnp.bfloat16):
    level = shard_levels(own_key, shape, pieces, -0.22, 0.18) if pieces else 1.0
    entries = jax.random.normal(own_key, shape, jnp.float32) * deviation * level
    return jnp.minimum(jnp.maximum(entries, -reach), reach).astype(kind)


def setup_inputs(seed: int = 0) -> dict:
    key_of = jax.random.split(jax.random.key(seed), 15)
    hidden_in = gaussian(key_of[0], (ROWS, D), 1.0, 6.0, ((0, 32),))
    norm_gain = jnp.clip(jnp.exp(jax.random.uniform(key_of[1], (D,), jnp.float32, math.log(0.25), math.log(4.0))), 0.25, 4.0)
    route_logits = gaussian(key_of[2], (ROWS, TOP), 1.5, 6.0, ((0, 32),), jnp.float32)
    expert_ids = draw_expert_ids(jax.random.fold_in(key_of[14], 71), 0)
    w_gate = gaussian(key_of[4], (WIN, D, MOE_FF), D ** -0.5, 0.0625, ((0, 4), (2, 8)))
    w_up = gaussian(key_of[5], (WIN, D, MOE_FF), D ** -0.5, 0.0625, ((0, 4), (2, 8)))
    w_down = gaussian(key_of[6], (WIN, MOE_FF, D), MOE_FF ** -0.5, 0.125, ((0, 4), (1, 8)))
    w_latent = gaussian(key_of[7], (D, KVW), D ** -0.5, 0.0625, ((0, 32),))
    kv_gain = jnp.clip(jnp.exp(jax.random.uniform(key_of[8], (LATENT,), jnp.float32, math.log(0.25), math.log(4.0))), 0.25, 4.0)
    queries = draw_queries(jax.random.fold_in(key_of[14], 71), 0)
    page_pool = gaussian(key_of[10], (POOLS, PAGE * KVW), 1.0, 6.0, ((0, 32),))
    page_table = plant(jax.random.randint(key_of[11], (ROWS, MAXP), 0, EXTENDED), jax.random.fold_in(key_of[11], 1), 0, EXTENDED - 1).astype(jnp.int32)
    kv_lengths = uneven(key_of[12], ROWS, ROWS * MAXP * PAGE // 2, MAXP * PAGE, 2).astype(jnp.int32)
    migration = plant(jax.random.randint(key_of[13], (N_DP, N_EXPERT, N_DP, MCAP), 0, POOL_DEV), jax.random.fold_in(key_of[13], 1), 0, POOL_DEV - 1).astype(jnp.int32)
    return {"hidden_in": hidden_in, "norm_gain": norm_gain, "route_logits": route_logits, "expert_ids": expert_ids, "w_gate": w_gate, "w_up": w_up, "w_down": w_down, "w_latent": w_latent, "kv_gain": kv_gain, "queries": queries, "page_pool": page_pool, "page_table": page_table, "kv_lengths": kv_lengths, "migration": migration}


softmax_scale = 192.0 ** (-0.5)
routed_scale = 2.5
norm_eps = 1e-06

def rms_rows(values, gain):
    stat = lax.optimization_barrier(jnp.mean(values * values, axis=-1, keepdims=True))
    return values * lax.rsqrt(stat + norm_eps) * gain

def rotate_keys(rope_part, position):
    half = ROPE // 2
    freq = 10000.0 ** (-jnp.arange(half, dtype=jnp.float32) / half)
    angle = position[:, None] * freq[None, :]
    first = rope_part[:, :half]
    second = rope_part[:, half:]
    cosine = jnp.cos(angle)
    sine = jnp.sin(angle)
    return jnp.concatenate([first * cosine - second * sine, second * cosine + first * sine], axis=1)

def reference(hidden_in, norm_gain, route_logits, expert_ids, w_gate, w_up, w_down, w_latent, kv_gain, queries, page_pool, page_table, kv_lengths, migration):
    devices = N_DP * N_EXPERT
    x_wide = hidden_in.astype(jnp.float32)
    normed = rms_rows(x_wide, norm_gain).astype(jnp.bfloat16)
    in_window = expert_ids < WIN
    has = jnp.any(in_window, axis=1)
    chosen = lax.optimization_barrier(jnp.sum(jnp.where(in_window, expert_ids, 0), axis=1)).astype(jnp.int32)
    sigma = jax.nn.sigmoid(route_logits)
    weight = routed_scale * lax.optimization_barrier(jnp.sum(jnp.where(in_window, sigma, 0.0), axis=1)) / lax.optimization_barrier(jnp.sum(sigma, axis=1))
    onehot = ((chosen[:, None] == jnp.arange(WIN, dtype=jnp.int32)[None, :]) & has[:, None]).astype(jnp.int32)
    onehot = onehot.reshape(devices, TOK_DEV, WIN)
    rank = jnp.cumsum(onehot, axis=1) - onehot
    slot = lax.optimization_barrier(jnp.sum(rank * onehot, axis=2)).reshape(ROWS).astype(jnp.int32)
    source = jnp.arange(ROWS, dtype=jnp.int32) // TOK_DEV
    column = (source * CAP + slot).astype(jnp.int32)
    target = jnp.where(has, chosen, WIN).astype(jnp.int32)
    buffers = jnp.zeros((WIN, devices * CAP, D), jnp.bfloat16).at[target, column].set(normed, mode='drop')

    def expert_apply(operands):
        rows_in, gate_w, up_w, down_w = operands
        gate = jnp.dot(rows_in, gate_w, preferred_element_type=jnp.float32)
        upper = jnp.dot(rows_in, up_w, preferred_element_type=jnp.float32)
        active = (jax.nn.silu(gate) * upper).astype(jnp.bfloat16)
        active = active.reshape(rows_in.shape[0], N_EXPERT, FF_DEV).astype(jnp.float32)
        down_parts = down_w.reshape(N_EXPERT, FF_DEV, D).astype(jnp.float32)
        partial_value = jnp.einsum('nsf,sfd->snd', active, down_parts, precision=lax.Precision.HIGHEST).astype(jnp.bfloat16)
        return lax.optimization_barrier(jnp.sum(partial_value.astype(jnp.float32), axis=0)).astype(jnp.bfloat16)
    outputs = lax.map(expert_apply, (buffers, w_gate, w_up, w_down))
    picked = outputs[jnp.minimum(chosen, WIN - 1), column].astype(jnp.float32)
    hidden_out = (x_wide + (weight * has.astype(jnp.float32))[:, None] * picked).astype(jnp.bfloat16)
    projected = jnp.dot(hidden_out, w_latent, preferred_element_type=jnp.float32)
    latent = rms_rows(projected[:, :LATENT], kv_gain)
    rotary = rotate_keys(projected[:, LATENT:], kv_lengths.astype(jnp.float32))
    new_key = jnp.concatenate([latent, rotary], axis=1).astype(jnp.bfloat16)
    dp_index = source // N_EXPERT
    ex_index = source % N_EXPERT
    own_page = page_table < POOL_DEV
    moved = jnp.maximum(page_table - POOL_DEV, 0)
    from_dp = moved // MCAP
    from_slot = moved % MCAP
    remote = migration[from_dp, ex_index[:, None], dp_index[:, None], from_slot]
    global_page = jnp.where(own_page, source[:, None] * POOL_DEV + page_table, (from_dp * N_EXPERT + ex_index[:, None]) * POOL_DEV + remote).astype(jnp.int32)

    def attend(operands):
        query_rows, pages, length, fresh = operands
        keys = page_pool[pages].reshape(TOK_DEV, MAXP * PAGE, KVW).astype(jnp.float32)
        query = query_rows.reshape(TOK_DEV, HEADS, KVW).astype(jnp.float32)
        fresh_wide = fresh.astype(jnp.float32)
        scores = jnp.einsum('rhc,rtc->rht', query, keys, precision=lax.Precision.HIGHEST) * softmax_scale
        own = jnp.einsum('rhc,rc->rh', query, fresh_wide, precision=lax.Precision.HIGHEST) * softmax_scale
        valid = jnp.arange(MAXP * PAGE, dtype=jnp.int32)[None, None, :] < length[:, None, None]
        top = jnp.maximum(lax.optimization_barrier(jnp.max(jnp.where(valid, scores, -1e+30), axis=2)), own)
        expo = jnp.where(valid, jnp.exp(scores - top[:, :, None]), 0.0)
        expo_own = jnp.exp(own - top)
        total = lax.optimization_barrier(jnp.sum(expo, axis=2)) + expo_own
        probs = (expo / total[:, :, None]).astype(jnp.bfloat16).astype(jnp.float32)
        probs_own = (expo_own / total).astype(jnp.bfloat16).astype(jnp.float32)
        result = jnp.einsum('rht,rtc->rhc', probs, keys[:, :, :LATENT], precision=lax.Precision.HIGHEST)
        result = result + probs_own[:, :, None] * fresh_wide[:, None, :LATENT]
        return result.astype(jnp.bfloat16).reshape(TOK_DEV, HEADS * LATENT)
    attended = lax.map(attend, (queries.reshape(devices, TOK_DEV, HEADS * KVW), global_page.reshape(devices, TOK_DEV, MAXP), kv_lengths.reshape(devices, TOK_DEV), new_key.reshape(devices, TOK_DEV, KVW)))
    return (hidden_out, attended.reshape(ROWS, HEADS * LATENT))
```

```python
import functools

import jax
import jax.numpy as jnp
from jax import lax
from jax.experimental import pallas as pl
from jax.experimental.pallas import tpu as pltpu
from jax.sharding import PartitionSpec as P

HEADS = 64
LATENT = 512
PAGE = 16
MAXP = 6
CAP = 4
MCAP = 4
KVW = 576


softmax_scale = 192.0 ** (-0.5)
routed_scale = 2.5
norm_eps = 1e-06


def rms_rows(values, gain):
    stat = jnp.mean(values * values, axis=-1, keepdims=True)
    return values * lax.rsqrt(stat + norm_eps) * gain


def rotate_keys(rope_part, position):
    half = rope_part.shape[1] // 2
    freq = 10000.0 ** (-jnp.arange(half, dtype=jnp.float32) / half)
    angle = position[:, None] * freq[None, :]
    first = rope_part[:, :half]
    second = rope_part[:, half:]
    cosine = jnp.cos(angle)
    sine = jnp.sin(angle)
    return jnp.concatenate([first * cosine - second * sine, second * cosine + first * sine], axis=1)


STEP = 512


def moe_kernel(
    dp, n, hid, gain, amap, bmap, wt, qmap, pmap, wg, wu, wd, out,
    wg_v, wu_v, wd_v, pack, arr, ret, xs, rs_r, rs_l, gacc, uacc, act,
    w_sem, a_send, a_recv, b_send, b_recv, agr_send, agr_recv, agl_send, agl_recv,
    rsr_send, rsr_recv, rsl_send, rsl_recv,
):
    f32 = jnp.float32
    bf16 = jnp.bfloat16
    me_d = lax.axis_index("dp")
    me_e = lax.axis_index("expert")
    mid = n // 2
    experts, width, _ = wg_v.shape
    half = width // 2
    steps = half // STEP
    block = xs.shape[2]
    rows_e = block // experts

    def ring_to_axis(p):
        return jnp.where(p < mid, 2 * p, 2 * (n - p) - 1)

    pos = jnp.where(lax.rem(me_e, 2) == 0, me_e // 2, n - (me_e + 1) // 2)
    right = (me_d, ring_to_axis(lax.rem(pos + 1, n)))
    left = (me_d, ring_to_axis(lax.rem(pos + n - 1, n)))

    def across(k):
        return (lax.rem(me_d + k, dp), me_e)

    weights = [
        pltpu.make_async_copy(a, b, w_sem.at[i])
        for i, (a, b) in enumerate(((wg, wg_v), (wu, wu_v), (wd, wd_v)))
    ]

    barrier = pltpu.get_barrier_semaphore()
    for device in [right, left] + [across(k) for k in range(1, dp)]:
        pl.semaphore_signal(
            barrier, inc=1, device_id=device, device_id_type=pl.DeviceIdType.MESH
        )

    def remote(src, dst, send, recv, device):
        return pltpu.make_async_remote_copy(
            src_ref=src,
            dst_ref=dst,
            send_sem=send,
            recv_sem=recv,
            device_id=device,
            device_id_type=pl.DeviceIdType.MESH,
        )

    def cols(i, base=0):
        return pl.ds(pl.multiple_of(base + i * STEP, STEP), STEP)

    def square(i, total):
        x = hid[:, cols(i)].astype(f32)
        return total + jnp.sum(x * x, axis=1, keepdims=True)

    stat = lax.fori_loop(0, 2 * steps, square, jnp.zeros((hid.shape[0], 1), f32)) / width
    scale = lax.rsqrt(stat + norm_eps)

    def pack_step(i, carry):
        total = None
        for h in range(2):
            c = cols(i, h * half)
            normed = (hid[:, c].astype(f32) * scale * gain[:, c]).astype(bf16)
            part = jnp.dot(amap[h], normed, preferred_element_type=f32)
            total = part if total is None else total + part
        total = total.astype(bf16).reshape(dp, 16, STEP)
        pack[:, :, cols(i)] = total
        arr[0, :, cols(i)] = total[0]
        return carry

    lax.fori_loop(0, steps, pack_step, 0)
    pl.semaphore_wait(barrier, dp + 1)
    there = [
        remote(pack.at[k], arr.at[k], a_send.at[k], a_recv.at[k], across(k)) for k in range(1, dp)
    ]
    for copy in there:
        copy.start()
    for copy in weights:
        copy.start()
    for copy in there:
        copy.wait()

    def sort_step(i, carry):
        rows = arr[:, :, cols(i)].reshape(dp * 16, STEP)
        for h in range(2):
            xs[0, h, :, cols(i)] = jnp.dot(qmap[h], rows, preferred_element_type=f32).astype(bf16)
        return carry

    lax.fori_loop(0, steps, sort_step, 0)

    def go_right(s, h):
        return remote(
            xs.at[s - 1, h], xs.at[s, h], agr_send.at[s - 1, h], agr_recv.at[s - 1, h], right
        )

    def go_left(s, h):
        return remote(
            xs.at[(n - s + 1) % n, h], xs.at[n - s, h], agl_send.at[s - 1, h],
            agl_recv.at[s - 1, h], left,
        )

    sent = []
    for s in range(1, mid + 1):
        for h in range(2):
            for go, last in ((go_right, 0), (go_left, 1)):
                if s > 1:
                    go(s - 1, h).wait_recv()
                if s < mid or h == last:
                    copy = go(s, h)
                    copy.start()
                    sent.append(copy)
    go_right(mid, 0).wait_recv()
    go_left(mid, 1).wait_recv()

    gacc[...] = jnp.zeros_like(gacc)
    uacc[...] = jnp.zeros_like(uacc)
    weights[0].wait()
    weights[1].wait()
    for h in range(2):

        def up_step(i, carry):
            for w in range(experts):
                rows = xs[:, h, w * rows_e : (w + 1) * rows_e, cols(i)].reshape(n * rows_e, STEP)
                k = cols(i, h * half)
                gacc[w] += jnp.dot(rows, wg_v[w, k, :], preferred_element_type=f32)
                uacc[w] += jnp.dot(rows, wu_v[w, k, :], preferred_element_type=f32)
            return carry

        lax.fori_loop(0, steps, up_step, 0)
    for w in range(experts):
        gate = gacc[w]
        act[w] = (gate / (1.0 + jnp.exp(-gate)) * uacc[w]).astype(bf16)
    for copy in sent:
        copy.wait_send()
    weights[2].wait()

    def back_right(s, h):
        return remote(
            xs.at[mid + s - 1, h], rs_r.at[s - 1, h], rsr_send.at[s - 1, h],
            rsr_recv.at[s - 1, h], right,
        )

    def back_left(s, h):
        return remote(
            xs.at[mid - s + 1, h], rs_l.at[s - 1, h], rsl_send.at[s - 1, h],
            rsl_recv.at[s - 1, h], left,
        )

    sent = []
    for h in range(2):

        def down_step(i, carry):
            for w in range(experts):
                part = jnp.dot(
                    act[w], wd_v[w, :, cols(i, h * half)], preferred_element_type=f32
                )
                xs[:, h, w * rows_e : (w + 1) * rows_e, cols(i)] = part.astype(bf16).reshape(
                    n, rows_e, STEP
                )
            return carry

        lax.fori_loop(0, steps, down_step, 0)
        for go in (back_right, back_left):
            if (go is back_right) == (h == 0):
                sent.append(go(1, h))
            else:
                sent.append(go(2, h))
            sent[-1].start()

    def add(slot, h, landed):
        def add_step(i, carry):
            c = cols(i)
            xs[slot, h, :, c] = (xs[slot, h, :, c].astype(f32) + landed[:, c].astype(f32)).astype(
                bf16
            )
            return carry

        lax.fori_loop(0, steps, add_step, 0)

    for s in range(2, mid + 1):
        for h in range(2):
            for go, first, slot, landing in (
                (back_right, 0, mid + s - 1, rs_r),
                (back_left, 1, mid - s + 1, rs_l),
            ):
                if s == 2 and h != first:
                    continue
                go(s - 1, h).wait_recv()
                add(slot, h, landing.at[s - 2, h])
                copy = go(s, h)
                copy.start()
                sent.append(copy)
    for h in range(2):
        back_right(mid, h).wait_recv()
        back_left(mid, h).wait_recv()

    def fold_step(i, carry):
        c = cols(i)
        total = None
        for h in range(2):
            mine = (
                xs[0, h, :, c].astype(f32)
                + rs_r[mid - 1, h, :, c].astype(f32)
                + rs_l[mid - 1, h, :, c].astype(f32)
            ).astype(bf16)
            part = jnp.dot(pmap[h], mine, preferred_element_type=f32)
            total = part if total is None else total + part
        total = total.astype(bf16).reshape(dp, 16, STEP)
        pack[:, :, c] = total
        ret[0, :, c] = total[0]
        return carry

    lax.fori_loop(0, steps, fold_step, 0)
    home = [
        remote(pack.at[k], ret.at[k], b_send.at[k], b_recv.at[k], across(dp - k))
        for k in range(1, dp)
    ]
    for copy in home:
        copy.start()
    for copy in home:
        copy.wait()

    def out_step(i, carry):
        rows = ret[:, :, cols(i)].reshape(dp * 16, STEP)
        for h in range(2):
            c = cols(i, h * half)
            picked = jnp.dot(bmap[h], rows, preferred_element_type=f32)
            out[:, c] = (hid[:, c].astype(f32) + wt[...] * picked).astype(bf16)
        return carry

    lax.fori_loop(0, steps, out_step, 0)
    for copy in sent:
        copy.wait_send()


def run_moe(dp, n, hidden_in, gain, amap, bmap, weight, qmap, pmap, w_gate, w_up, w_down):
    rows, width = hidden_in.shape
    experts, _, units = w_gate.shape
    half = width // 2
    mid = n // 2
    block = experts * dp * CAP
    bf16 = jnp.bfloat16
    dma = pltpu.SemaphoreType.DMA
    vmem = pl.BlockSpec(memory_space=pltpu.VMEM)
    hbm = pl.BlockSpec(memory_space=pl.ANY)
    return pl.pallas_call(
        functools.partial(moe_kernel, dp, n),
        out_shape=jax.ShapeDtypeStruct((rows, width), bf16),
        in_specs=[vmem] * 7 + [hbm] * 3,
        out_specs=vmem,
        scratch_shapes=[
            pltpu.VMEM((experts, width, units), bf16),
            pltpu.VMEM((experts, width, units), bf16),
            pltpu.VMEM((experts, units, width), bf16),
            pltpu.VMEM((dp, 16, half), bf16),
            pltpu.VMEM((dp, 16, half), bf16),
            pltpu.VMEM((dp, 16, half), bf16),
            pltpu.VMEM((n, 2, block, half), bf16),
            pltpu.VMEM((mid, 2, block, half), bf16),
            pltpu.VMEM((mid, 2, block, half), bf16),
            pltpu.VMEM((experts, n * block // experts, units), jnp.float32),
            pltpu.VMEM((experts, n * block // experts, units), jnp.float32),
            pltpu.VMEM((experts, n * block // experts, units), bf16),
            dma((3,)),
            dma((dp,)),
            dma((dp,)),
            dma((dp,)),
            dma((dp,)),
        ]
        + [dma((mid, 2))] * 8,
        compiler_params=pltpu.CompilerParams(
            collective_id=0, has_side_effects=True, vmem_limit_bytes=60 * 2**20
        ),
        cost_estimate=pl.CostEstimate(
            flops=6 * n * block * width * units,
            bytes_accessed=6 * experts * width * units,
            transcendentals=n * block * units,
        ),
        name="experts",
    )(hidden_in, gain, amap, bmap, weight, qmap, pmap, w_gate, w_up, w_down)


def body(
    hidden_in,
    norm_gain,
    route_logits,
    expert_ids,
    w_gate,
    w_up,
    w_down,
    w_latent,
    kv_gain,
    queries,
    page_pool,
    page_table,
    kv_lengths,
    migration,
):
    dp_count = lax.axis_size("dp")
    row_count = hidden_in.shape[0]
    local_experts = w_gate.shape[0]
    window = local_experts * dp_count
    flat_list = migration.reshape(dp_count * MCAP)
    outgoing = jnp.take(page_pool, flat_list, axis=0).reshape(dp_count, MCAP, page_pool.shape[1])
    incoming = lax.all_to_all(outgoing, "dp", split_axis=0, concat_axis=0, tiled=True)
    in_window = expert_ids < window
    has = jnp.any(in_window, axis=1)
    chosen = jnp.sum(jnp.where(in_window, expert_ids, 0), axis=1)
    sigma = jax.nn.sigmoid(route_logits)
    weight = (
        routed_scale * jnp.sum(jnp.where(in_window, sigma, 0.0), axis=1) / jnp.sum(sigma, axis=1)
    )
    onehot = ((chosen[:, None] == jnp.arange(window)[None, :]) & has[:, None]).astype(jnp.int32)
    rank = jnp.cumsum(onehot, axis=0) - onehot
    slot = jnp.sum(rank * onehot, axis=1)
    group = chosen // local_experts
    within = chosen % local_experts
    apart = (group - lax.axis_index("dp") + dp_count) % dp_count
    halves = jnp.arange(2)[:, None, None]
    target = apart * 16 + within * CAP + slot
    lines = jnp.arange(dp_count * 16)
    hit = (target[None, :, None] + 8 * halves == lines[None, None, :]) & has[None, :, None]
    back_map = hit.astype(jnp.bfloat16)
    send_map = jnp.swapaxes(back_map, 1, 2)
    block = local_experts * dp_count * CAP
    places = jnp.arange(block)
    own_expert = places // (dp_count * CAP)
    source = places // CAP % dp_count
    origin = source * 16 + own_expert * CAP + places % CAP
    sort_map = (origin[None, :, None] + 8 * halves == lines[None, None, :]).astype(jnp.bfloat16)
    hidden_out = run_moe(
        dp_count,
        lax.axis_size("expert"),
        hidden_in,
        norm_gain[None, :],
        send_map,
        back_map,
        jnp.where(has, weight, 0.0)[:, None],
        sort_map,
        jnp.swapaxes(sort_map, 1, 2),
        w_gate,
        w_up,
        w_down,
    )
    projected = jnp.dot(
        hidden_out,
        lax.all_gather(w_latent, ("dp", "expert"), axis=0, tiled=True),
        preferred_element_type=jnp.float32,
    )
    latent = rms_rows(projected[:, :LATENT], kv_gain)
    rotary = rotate_keys(projected[:, LATENT:], kv_lengths.astype(jnp.float32))
    new_key = jnp.concatenate([latent, rotary], axis=1).astype(jnp.bfloat16)
    extended = jnp.concatenate(
        [page_pool, incoming.reshape(dp_count * MCAP, page_pool.shape[1])], axis=0
    )
    keys = jnp.take(extended, page_table.reshape(row_count * MAXP), axis=0).reshape(
        row_count, MAXP * PAGE, KVW
    )
    query = queries.reshape(row_count, HEADS, KVW)
    scores = (
        jnp.einsum("rhc,rtc->rht", query, keys, preferred_element_type=jnp.float32) * softmax_scale
    )
    own = (
        jnp.einsum("rhc,rc->rh", query, new_key, preferred_element_type=jnp.float32) * softmax_scale
    )
    valid = jnp.arange(MAXP * PAGE)[None, None, :] < kv_lengths[:, None, None]
    top = jnp.maximum(jnp.max(jnp.where(valid, scores, -1e30), axis=2), own)
    expo = jnp.where(valid, jnp.exp(scores - top[:, :, None]), 0.0)
    expo_own = jnp.exp(own - top)
    total = jnp.sum(expo, axis=2) + expo_own
    probs = (expo / total[:, :, None]).astype(jnp.bfloat16)
    probs_own = (expo_own / total).astype(jnp.bfloat16)
    result = jnp.einsum(
        "rht,rtc->rhc", probs, keys[:, :, :LATENT], preferred_element_type=jnp.float32
    )
    result = result + probs_own.astype(jnp.float32)[:, :, None] * new_key[:, None, :LATENT].astype(
        jnp.float32
    )
    attended = result.astype(jnp.bfloat16).reshape(row_count, HEADS * LATENT)
    return (hidden_out, attended)


def solution(mesh):
    return jax.shard_map(
        body,
        mesh=mesh,
        in_specs=(
            P(("dp", "expert"), None),
            P(),
            P(("dp", "expert"), None),
            P(("dp", "expert"), None),
            P("dp", None, "expert"),
            P("dp", None, "expert"),
            P("dp", "expert", None),
            P(("dp", "expert"), None),
            P(),
            P(("dp", "expert"), None),
            P(("dp", "expert"), None),
            P(("dp", "expert"), None),
            P(("dp", "expert")),
            P("dp", "expert", None, None),
        ),
        out_specs=(P(("dp", "expert"), None), P(("dp", "expert"), None)),
        check_vma=False,
    )
```

```python
import functools

import jax
import jax.numpy as jnp
from jax import lax
from jax.experimental import pallas as pl
from jax.experimental.pallas import tpu as pltpu
from jax.sharding import PartitionSpec as P

HEADS = 64
LATENT = 512
PAGE = 16
MAXP = 6
CAP = 4
MCAP = 4
KVW = 576


softmax_scale = 192.0 ** (-0.5)
routed_scale = 2.5
norm_eps = 1e-06


def rms_rows(values, gain):
    stat = jnp.mean(values * values, axis=-1, keepdims=True)
    return values * lax.rsqrt(stat + norm_eps) * gain


def rotate_keys(rope_part, position):
    half = rope_part.shape[1] // 2
    freq = 10000.0 ** (-jnp.arange(half, dtype=jnp.float32) / half)
    angle = position[:, None] * freq[None, :]
    first = rope_part[:, :half]
    second = rope_part[:, half:]
    cosine = jnp.cos(angle)
    sine = jnp.sin(angle)
    return jnp.concatenate([first * cosine - second * sine, second * cosine + first * sine], axis=1)


STEP = 512


def moe_kernel(
    dp, n, hid, gain, amap, bmap, wt, qmap, pmap, wg, wu, wd, out,
    wg_v, wu_v, wd_v, pack, arr, ret, xs, rs_r, rs_l, gacc, uacc, act,
    w_sem, a_send, a_recv, b_send, b_recv, agr_send, agr_recv, agl_send, agl_recv,
    rsr_send, rsr_recv, rsl_send, rsl_recv,
):
    f32 = jnp.float32
    bf16 = jnp.bfloat16
    me_d = lax.axis_index("dp")
    me_e = lax.axis_index("expert")
    mid = n // 2
    experts, width, _ = wg_v.shape
    half = width // 2
    steps = half // STEP
    block = xs.shape[2]
    rows_e = block // experts

    def ring_to_axis(p):
        return jnp.where(p < mid, 2 * p, 2 * (n - p) - 1)

    pos = jnp.where(lax.rem(me_e, 2) == 0, me_e // 2, n - (me_e + 1) // 2)
    right = (me_d, ring_to_axis(lax.rem(pos + 1, n)))
    left = (me_d, ring_to_axis(lax.rem(pos + n - 1, n)))

    def across(k):
        return (lax.rem(me_d + k, dp), me_e)

    weights = [
        pltpu.make_async_copy(a, b, w_sem.at[i])
        for i, (a, b) in enumerate(((wg, wg_v), (wu, wu_v), (wd, wd_v)))
    ]

    barrier = pltpu.get_barrier_semaphore()
    for device in [right, left] + [across(k) for k in range(1, dp)]:
        pl.semaphore_signal(
            barrier, inc=1, device_id=device, device_id_type=pl.DeviceIdType.MESH
        )

    def remote(src, dst, send, recv, device):
        return pltpu.make_async_remote_copy(
            src_ref=src,
            dst_ref=dst,
            send_sem=send,
            recv_sem=recv,
            device_id=device,
            device_id_type=pl.DeviceIdType.MESH,
        )

    def cols(i, base=0):
        return pl.ds(pl.multiple_of(base + i * STEP, STEP), STEP)

    def square(i, total):
        x = hid[:, cols(i)].astype(f32)
        return total + jnp.sum(x * x, axis=1, keepdims=True)

    stat = lax.fori_loop(0, 2 * steps, square, jnp.zeros((hid.shape[0], 1), f32)) / width
    scale = lax.rsqrt(stat + norm_eps)

    def pack_step(i, carry):
        total = None
        for h in range(2):
            c = cols(i, h * half)
            normed = (hid[:, c].astype(f32) * scale * gain[:, c]).astype(bf16)
            part = jnp.dot(amap[h], normed, preferred_element_type=f32)
            total = part if total is None else total + part
        total = total.astype(bf16).reshape(dp, 16, STEP)
        pack[:, :, cols(i)] = total
        arr[0, :, cols(i)] = total[0]
        return carry

    lax.fori_loop(0, steps, pack_step, 0)
    pl.semaphore_wait(barrier, dp + 1)
    there = [
        remote(pack.at[k], arr.at[k], a_send.at[k], a_recv.at[k], across(k)) for k in range(1, dp)
    ]
    for copy in there:
        copy.start()
    for copy in weights:
        copy.start()
    for copy in there:
        copy.wait()

    def sort_step(i, carry):
        rows = arr[:, :, cols(i)].reshape(dp * 16, STEP)
        for h in range(2):
            xs[0, h, :, cols(i)] = jnp.dot(qmap[h], rows, preferred_element_type=f32).astype(bf16)
        return carry

    lax.fori_loop(0, steps, sort_step, 0)

    def go_right(s, h):
        return remote(
            xs.at[s - 1, h], xs.at[s, h], agr_send.at[s - 1, h], agr_recv.at[s - 1, h], right
        )

    def go_left(s, h):
        return remote(
            xs.at[(n - s + 1) % n, h], xs.at[n - s, h], agl_send.at[s - 1, h],
            agl_recv.at[s - 1, h], left,
        )

    sent = []
    for s in range(1, mid + 1):
        for h in range(2):
            for go, last in ((go_right, 0), (go_left, 1)):
                if s > 1:
                    go(s - 1, h).wait_recv()
                if s < mid or h == last:
                    copy = go(s, h)
                    copy.start()
                    sent.append(copy)
    go_right(mid, 0).wait_recv()
    go_left(mid, 1).wait_recv()

    gacc[...] = jnp.zeros_like(gacc)
    uacc[...] = jnp.zeros_like(uacc)
    weights[0].wait()
    weights[1].wait()
    for h in range(2):

        def up_step(i, carry):
            for w in range(experts):
                rows = xs[:, h, w * rows_e : (w + 1) * rows_e, cols(i)].reshape(n * rows_e, STEP)
                k = cols(i, h * half)
                gacc[w] += jnp.dot(rows, wg_v[w, k, :], preferred_element_type=f32)
                uacc[w] += jnp.dot(rows, wu_v[w, k, :], preferred_element_type=f32)
            return carry

        lax.fori_loop(0, steps, up_step, 0)
    for w in range(experts):
        gate = gacc[w]
        act[w] = (gate / (1.0 + jnp.exp(-gate)) * uacc[w]).astype(bf16)
    for copy in sent:
        copy.wait_send()
    weights[2].wait()

    def back_right(s, h):
        return remote(
            xs.at[mid + s - 1, h], rs_r.at[s - 1, h], rsr_send.at[s - 1, h],
            rsr_recv.at[s - 1, h], right,
        )

    def back_left(s, h):
        return remote(
            xs.at[mid - s + 1, h], rs_l.at[s - 1, h], rsl_send.at[s - 1, h],
            rsl_recv.at[s - 1, h], left,
        )

    sent = []
    for h in range(2):

        def down_step(i, carry):
            for w in range(experts):
                part = jnp.dot(
                    act[w], wd_v[w, :, cols(i, h * half)], preferred_element_type=f32
                )
                xs[:, h, w * rows_e : (w + 1) * rows_e, cols(i)] = part.astype(bf16).reshape(
                    n, rows_e, STEP
                )
            return carry

        lax.fori_loop(0, steps, down_step, 0)
        for go in (back_right, back_left):
            if (go is back_right) == (h == 0):
                sent.append(go(1, h))
            else:
                sent.append(go(2, h))
            sent[-1].start()

    def add(slot, h, landed):
        def add_step(i, carry):
            c = cols(i)
            xs[slot, h, :, c] = (xs[slot, h, :, c].astype(f32) + landed[:, c].astype(f32)).astype(
                bf16
            )
            return carry

        lax.fori_loop(0, steps, add_step, 0)

    for s in range(2, mid + 1):
        for h in range(2):
            for go, first, slot, landing in (
                (back_right, 0, mid + s - 1, rs_r),
                (back_left, 1, mid - s + 1, rs_l),
            ):
                if s == 2 and h != first:
                    continue
                go(s - 1, h).wait_recv()
                add(slot, h, landing.at[s - 2, h])
                copy = go(s, h)
                copy.start()
                sent.append(copy)
    for h in range(2):
        back_right(mid, h).wait_recv()
        back_left(mid, h).wait_recv()

    def fold_step(i, carry):
        c = cols(i)
        total = None
        for h in range(2):
            mine = (
                xs[0, h, :, c].astype(f32)
                + rs_r[mid - 1, h, :, c].astype(f32)
                + rs_l[mid - 1, h, :, c].astype(f32)
            ).astype(bf16)
            part = jnp.dot(pmap[h], mine, preferred_element_type=f32)
            total = part if total is None else total + part
        total = total.astype(bf16).reshape(dp, 16, STEP)
        pack[:, :, c] = total
        ret[0, :, c] = total[0]
        return carry

    lax.fori_loop(0, steps, fold_step, 0)
    home = [
        remote(pack.at[k], ret.at[k], b_send.at[k], b_recv.at[k], across(dp - k))
        for k in range(1, dp)
    ]
    for copy in home:
        copy.start()
    for copy in home:
        copy.wait()

    def out_step(i, carry):
        rows = ret[:, :, cols(i)].reshape(dp * 16, STEP)
        for h in range(2):
            c = cols(i, h * half)
            picked = jnp.dot(bmap[h], rows, preferred_element_type=f32)
            out[:, c] = (hid[:, c].astype(f32) + wt[...] * picked).astype(bf16)
        return carry

    lax.fori_loop(0, steps, out_step, 0)
    for copy in sent:
        copy.wait_send()


def run_moe(dp, n, hidden_in, gain, amap, bmap, weight, qmap, pmap, w_gate, w_up, w_down):
    rows, width = hidden_in.shape
    experts, _, units = w_gate.shape
    half = width // 2
    mid = n // 2
    block = experts * dp * CAP
    bf16 = jnp.bfloat16
    dma = pltpu.SemaphoreType.DMA
    vmem = pl.BlockSpec(memory_space=pltpu.VMEM)
    hbm = pl.BlockSpec(memory_space=pl.ANY)
    return pl.pallas_call(
        functools.partial(moe_kernel, dp, n),
        out_shape=jax.ShapeDtypeStruct((rows, width), bf16),
        in_specs=[vmem] * 7 + [hbm] * 3,
        out_specs=vmem,
        scratch_shapes=[
            pltpu.VMEM((experts, width, units), bf16),
            pltpu.VMEM((experts, width, units), bf16),
            pltpu.VMEM((experts, units, width), bf16),
            pltpu.VMEM((dp, 16, half), bf16),
            pltpu.VMEM((dp, 16, half), bf16),
            pltpu.VMEM((dp, 16, half), bf16),
            pltpu.VMEM((n, 2, block, half), bf16),
            pltpu.VMEM((mid, 2, block, half), bf16),
            pltpu.VMEM((mid, 2, block, half), bf16),
            pltpu.VMEM((experts, n * block // experts, units), jnp.float32),
            pltpu.VMEM((experts, n * block // experts, units), jnp.float32),
            pltpu.VMEM((experts, n * block // experts, units), bf16),
            dma((3,)),
            dma((dp,)),
            dma((dp,)),
            dma((dp,)),
            dma((dp,)),
        ]
        + [dma((mid, 2))] * 8,
        compiler_params=pltpu.CompilerParams(
            collective_id=0, has_side_effects=True, vmem_limit_bytes=60 * 2**20
        ),
        cost_estimate=pl.CostEstimate(
            flops=6 * n * block * width * units,
            bytes_accessed=6 * experts * width * units,
            transcendentals=n * block * units,
        ),
        name="experts",
    )(hidden_in, gain, amap, bmap, weight, qmap, pmap, w_gate, w_up, w_down)


PAD = 640
TABLE = 256
SPAN = 896


def attend_kernel(q, pick, bias, fresh, pool, moved, out, pages, keys, qs, outs):
    f32 = jnp.float32
    bf16 = jnp.bfloat16
    groups = keys.shape[0]
    listed = MAXP * 8
    cached = listed * PAGE
    pairs = HEADS // 2
    extended = pool.shape[0] + moved.shape[0]

    @pl.when(pl.program_id(0) == 0)
    def _():
        pages[...] = jnp.zeros_like(pages)
        keys[:, cached:, :] = jnp.zeros((groups, SPAN - cached, PAD), bf16)
        keys[:, cached : cached + 16, :] = fresh[...]
        lane = lax.broadcasted_iota(jnp.int32, (extended, PAD), 1)

        def window(start):
            c = pl.ds(pl.multiple_of(start, 128), PAD)
            return jnp.concatenate([pool[:, c].astype(f32), moved[:, c].astype(f32)], axis=0)

        def split(i, carry):
            even = jnp.where(lane < KVW, window(i * (2 * KVW)), 0.0)
            odd = jnp.where(lane >= PAD - KVW, window(i * (2 * KVW) + 2 * KVW - PAD), 0.0)
            pages[2 * i, :extended, :] = even.astype(bf16)
            pages[2 * i + 1, :extended, :] = pltpu.roll(odd, KVW, 1).astype(bf16)
            return carry

        lax.fori_loop(0, PAGE // 2, split, 0)

        def gather(u, carry):
            rows = jnp.dot(pick[...], pages[u], preferred_element_type=f32).astype(bf16)
            keys[:, pl.ds(pl.multiple_of(u * listed, 16), listed), :] = rows.reshape(
                groups, listed, PAD
            )
            return carry

        lax.fori_loop(0, PAGE, gather, 0)

    for odd in range(2):

        def load(i, carry):
            start = pl.multiple_of(i * (2 * KVW) + odd * (2 * KVW - PAD), 128)
            x = q[:, pl.ds(start, PAD)].astype(f32)
            if odd:
                x = pltpu.roll(x, KVW, 1)
            at = pl.ds(pl.multiple_of(i * 8, 8), 8)
            qs[0, at, :] = x[:8]
            qs[1, at, :] = x[8:]
            return carry

        lax.fori_loop(0, pairs, load, 0)
        for sub in range(2):
            group = pl.program_id(0) * 2 + sub
            scores = lax.dot_general(
                qs[sub].astype(bf16),
                keys[group],
                (((1,), (1,)), ((), ())),
                preferred_element_type=f32,
            )
            scores = (
                scores.reshape(pairs, 8, SPAN) * softmax_scale
                + bias[sub * 8 : sub * 8 + 8, :][None]
            )
            top = jnp.max(scores, axis=2, keepdims=True)
            expo = jnp.exp(scores - top)
            total = jnp.sum(expo, axis=2, keepdims=True)
            probs = (expo * (1.0 / total)).reshape(pairs * 8, SPAN).astype(bf16)
            outs[sub] = jnp.dot(probs, keys[group, :, :LATENT], preferred_element_type=f32)

        def store(i, carry):
            at = pl.ds(pl.multiple_of(i * 8, 8), 8)
            rows = jnp.concatenate([outs[0, at, :], outs[1, at, :]], axis=0)
            start = pl.multiple_of(i * (2 * LATENT) + odd * LATENT, 128)
            out[:, pl.ds(start, LATENT)] = rows.astype(bf16)
            return carry

        lax.fori_loop(0, pairs, store, 0)


def run_attend(queries, page_table, kv_lengths, new_key, page_pool, moved):
    rows = queries.shape[0]
    groups = rows // 8
    listed = MAXP * 8
    bf16 = jnp.bfloat16
    pick = (page_table.reshape(rows * MAXP)[:, None] == jnp.arange(TABLE)[None, :]).astype(bf16)
    place = jnp.arange(SPAN)
    entry = place % listed
    owner = jnp.where(place < listed * PAGE, entry // MAXP, place - listed * PAGE)
    time = jnp.where(place < listed * PAGE, entry % MAXP * PAGE + place // listed, -1)
    mine = (jnp.arange(rows) % 8)[:, None] == owner[None, :]
    bias = jnp.where(mine & (time[None, :] < kv_lengths[:, None]), 0.0, -1e30)
    fresh = jnp.pad(new_key.reshape(groups, 8, KVW), ((0, 0), (0, 8), (0, PAD - KVW)))

    def whole(array):
        return pl.BlockSpec(array.shape, lambda i: (0,) * array.ndim)

    return pl.pallas_call(
        attend_kernel,
        grid=(rows // 16,),
        out_shape=jax.ShapeDtypeStruct((rows, HEADS * LATENT), bf16),
        in_specs=[
            pl.BlockSpec((16, HEADS * KVW), lambda i: (i, 0)),
            whole(pick),
            pl.BlockSpec((16, SPAN), lambda i: (i, 0)),
            whole(fresh),
            whole(page_pool),
            whole(moved),
        ],
        out_specs=pl.BlockSpec((16, HEADS * LATENT), lambda i: (i, 0)),
        scratch_shapes=[
            pltpu.VMEM((PAGE, TABLE, PAD), bf16),
            pltpu.VMEM((groups, SPAN, PAD), bf16),
            pltpu.VMEM((2, HEADS * 4, PAD), jnp.float32),
            pltpu.VMEM((2, HEADS * 4, LATENT), jnp.float32),
        ],
        compiler_params=pltpu.CompilerParams(vmem_limit_bytes=56 * 2**20),
        cost_estimate=pl.CostEstimate(
            flops=4 * rows * HEADS * SPAN * PAD,
            bytes_accessed=2 * rows * HEADS * (KVW + LATENT),
            transcendentals=rows * HEADS * SPAN,
        ),
        name="attend",
    )(queries, pick, bias, fresh, page_pool, moved)


def body(
    hidden_in,
    norm_gain,
    route_logits,
    expert_ids,
    w_gate,
    w_up,
    w_down,
    w_latent,
    kv_gain,
    queries,
    page_pool,
    page_table,
    kv_lengths,
    migration,
):
    dp_count = lax.axis_size("dp")
    local_experts = w_gate.shape[0]
    window = local_experts * dp_count
    flat_list = migration.reshape(dp_count * MCAP)
    outgoing = jnp.take(page_pool, flat_list, axis=0).reshape(dp_count, MCAP, page_pool.shape[1])
    incoming = lax.all_to_all(outgoing, "dp", split_axis=0, concat_axis=0, tiled=True)
    in_window = expert_ids < window
    has = jnp.any(in_window, axis=1)
    chosen = jnp.sum(jnp.where(in_window, expert_ids, 0), axis=1)
    sigma = jax.nn.sigmoid(route_logits)
    weight = (
        routed_scale * jnp.sum(jnp.where(in_window, sigma, 0.0), axis=1) / jnp.sum(sigma, axis=1)
    )
    onehot = ((chosen[:, None] == jnp.arange(window)[None, :]) & has[:, None]).astype(jnp.int32)
    rank = jnp.cumsum(onehot, axis=0) - onehot
    slot = jnp.sum(rank * onehot, axis=1)
    group = chosen // local_experts
    within = chosen % local_experts
    apart = (group - lax.axis_index("dp") + dp_count) % dp_count
    halves = jnp.arange(2)[:, None, None]
    target = apart * 16 + within * CAP + slot
    lines = jnp.arange(dp_count * 16)
    hit = (target[None, :, None] + 8 * halves == lines[None, None, :]) & has[None, :, None]
    back_map = hit.astype(jnp.bfloat16)
    send_map = jnp.swapaxes(back_map, 1, 2)
    block = local_experts * dp_count * CAP
    places = jnp.arange(block)
    own_expert = places // (dp_count * CAP)
    source = places // CAP % dp_count
    origin = source * 16 + own_expert * CAP + places % CAP
    sort_map = (origin[None, :, None] + 8 * halves == lines[None, None, :]).astype(jnp.bfloat16)
    hidden_out = run_moe(
        dp_count,
        lax.axis_size("expert"),
        hidden_in,
        norm_gain[None, :],
        send_map,
        back_map,
        jnp.where(has, weight, 0.0)[:, None],
        sort_map,
        jnp.swapaxes(sort_map, 1, 2),
        w_gate,
        w_up,
        w_down,
    )
    latent_part = lax.all_gather(w_latent, "expert", axis=0, tiled=True)
    features = lax.all_to_all(hidden_out, "dp", split_axis=1, concat_axis=0, tiled=True)
    products = jnp.dot(features, latent_part, preferred_element_type=jnp.float32)
    products = lax.all_to_all(products, "dp", split_axis=0, concat_axis=0, tiled=True)
    projected = jnp.sum(products.reshape(dp_count, hidden_in.shape[0], KVW), axis=0)
    latent = rms_rows(projected[:, :LATENT], kv_gain)
    rotary = rotate_keys(projected[:, LATENT:], kv_lengths.astype(jnp.float32))
    new_key = jnp.concatenate([latent, rotary], axis=1).astype(jnp.bfloat16)
    moved = incoming.reshape(dp_count * MCAP, page_pool.shape[1])
    attended = run_attend(queries, page_table, kv_lengths, new_key, page_pool, moved)
    return (hidden_out, attended)


def solution(mesh):
    return jax.shard_map(
        body,
        mesh=mesh,
        in_specs=(
            P(("dp", "expert"), None),
            P(),
            P(("dp", "expert"), None),
            P(("dp", "expert"), None),
            P("dp", None, "expert"),
            P("dp", None, "expert"),
            P("dp", "expert", None),
            P(("dp", "expert"), None),
            P(),
            P(("dp", "expert"), None),
            P(("dp", "expert"), None),
            P(("dp", "expert"), None),
            P(("dp", "expert")),
            P("dp", "expert", None, None),
        ),
        out_specs=(P(("dp", "expert"), None), P(("dp", "expert"), None)),
        check_vma=False,
    )
```

```python
import functools

import jax
import jax.numpy as jnp
from jax import lax
from jax.experimental import pallas as pl
from jax.experimental.pallas import tpu as pltpu
from jax.sharding import PartitionSpec as P

HEADS = 64
LATENT = 512
PAGE = 16
MAXP = 6
CAP = 4
MCAP = 4
KVW = 576


softmax_scale = 192.0 ** (-0.5)
routed_scale = 2.5
norm_eps = 1e-06


def rms_rows(values, gain):
    stat = jnp.mean(values * values, axis=-1, keepdims=True)
    return values * lax.rsqrt(stat + norm_eps) * gain


def rotate_keys(rope_part, position):
    half = rope_part.shape[1] // 2
    freq = 10000.0 ** (-jnp.arange(half, dtype=jnp.float32) / half)
    angle = position[:, None] * freq[None, :]
    first = rope_part[:, :half]
    second = rope_part[:, half:]
    cosine = jnp.cos(angle)
    sine = jnp.sin(angle)
    return jnp.concatenate([first * cosine - second * sine, second * cosine + first * sine], axis=1)


STEP = 512


def moe_kernel(
    dp, n, hid, gain, amap, bmap, wt, qmap, pmap, wg, wu, wd, out,
    wg_v, wu_v, wd_v, pack, arr, ret, xs, rs_r, rs_l, gacc, uacc, act,
    w_sem, a_send, a_recv, b_send, b_recv, agr_send, agr_recv, agl_send, agl_recv,
    rsr_send, rsr_recv, rsl_send, rsl_recv,
):
    f32 = jnp.float32
    bf16 = jnp.bfloat16
    me_d = lax.axis_index("dp")
    me_e = lax.axis_index("expert")
    mid = n // 2
    experts, width, _ = wg_v.shape
    half = width // 2
    steps = half // STEP
    block = xs.shape[2]
    rows_e = block // experts

    def ring_to_axis(p):
        return jnp.where(p < mid, 2 * p, 2 * (n - p) - 1)

    pos = jnp.where(lax.rem(me_e, 2) == 0, me_e // 2, n - (me_e + 1) // 2)
    right = (me_d, ring_to_axis(lax.rem(pos + 1, n)))
    left = (me_d, ring_to_axis(lax.rem(pos + n - 1, n)))

    def across(k):
        return (lax.rem(me_d + k, dp), me_e)

    weights = [
        pltpu.make_async_copy(a, b, w_sem.at[i])
        for i, (a, b) in enumerate(((wg, wg_v), (wu, wu_v), (wd, wd_v)))
    ]

    barrier = pltpu.get_barrier_semaphore()
    for device in [right, left] + [across(k) for k in range(1, dp)]:
        pl.semaphore_signal(
            barrier, inc=1, device_id=device, device_id_type=pl.DeviceIdType.MESH
        )

    def remote(src, dst, send, recv, device):
        return pltpu.make_async_remote_copy(
            src_ref=src,
            dst_ref=dst,
            send_sem=send,
            recv_sem=recv,
            device_id=device,
            device_id_type=pl.DeviceIdType.MESH,
        )

    def cols(i, base=0):
        return pl.ds(pl.multiple_of(base + i * STEP, STEP), STEP)

    def square(i, total):
        x = hid[:, cols(i)].astype(f32)
        return total + jnp.sum(x * x, axis=1, keepdims=True)

    stat = lax.fori_loop(0, 2 * steps, square, jnp.zeros((hid.shape[0], 1), f32)) / width
    scale = lax.rsqrt(stat + norm_eps)

    def pack_step(i, carry):
        total = None
        for h in range(2):
            c = cols(i, h * half)
            normed = (hid[:, c].astype(f32) * scale * gain[:, c]).astype(bf16)
            part = jnp.dot(amap[h], normed, preferred_element_type=f32)
            total = part if total is None else total + part
        total = total.astype(bf16).reshape(dp, 16, STEP)
        pack[:, :, cols(i)] = total
        arr[0, :, cols(i)] = total[0]
        return carry

    lax.fori_loop(0, steps, pack_step, 0)
    pl.semaphore_wait(barrier, dp + 1)
    there = [
        remote(pack.at[k], arr.at[k], a_send.at[k], a_recv.at[k], across(k)) for k in range(1, dp)
    ]
    for copy in there:
        copy.start()
    for copy in weights:
        copy.start()
    for copy in there:
        copy.wait()

    def sort_step(i, carry):
        rows = arr[:, :, cols(i)].reshape(dp * 16, STEP)
        for h in range(2):
            xs[0, h, :, cols(i)] = jnp.dot(qmap[h], rows, preferred_element_type=f32).astype(bf16)
        return carry

    lax.fori_loop(0, steps, sort_step, 0)

    def go_right(s, h):
        return remote(
            xs.at[s - 1, h], xs.at[s, h], agr_send.at[s - 1, h], agr_recv.at[s - 1, h], right
        )

    def go_left(s, h):
        return remote(
            xs.at[(n - s + 1) % n, h], xs.at[n - s, h], agl_send.at[s - 1, h],
            agl_recv.at[s - 1, h], left,
        )

    sent = []
    for s in range(1, mid + 1):
        for h in range(2):
            for go, last in ((go_right, 0), (go_left, 1)):
                if s > 1:
                    go(s - 1, h).wait_recv()
                if s < mid or h == last:
                    copy = go(s, h)
                    copy.start()
                    sent.append(copy)
    go_right(mid, 0).wait_recv()
    go_left(mid, 1).wait_recv()

    gacc[...] = jnp.zeros_like(gacc)
    uacc[...] = jnp.zeros_like(uacc)
    weights[0].wait()
    weights[1].wait()
    for h in range(2):

        def up_step(i, carry):
            for w in range(experts):
                rows = xs[:, h, w * rows_e : (w + 1) * rows_e, cols(i)].reshape(n * rows_e, STEP)
                k = cols(i, h * half)
                gacc[w] += jnp.dot(rows, wg_v[w, k, :], preferred_element_type=f32)
                uacc[w] += jnp.dot(rows, wu_v[w, k, :], preferred_element_type=f32)
            return carry

        lax.fori_loop(0, steps, up_step, 0)
    for w in range(experts):
        gate = gacc[w]
        act[w] = (gate / (1.0 + jnp.exp(-gate)) * uacc[w]).astype(bf16)
    for copy in sent:
        copy.wait_send()
    weights[2].wait()

    def back_right(s, h):
        return remote(
            xs.at[mid + s - 1, h], rs_r.at[s - 1, h], rsr_send.at[s - 1, h],
            rsr_recv.at[s - 1, h], right,
        )

    def back_left(s, h):
        return remote(
            xs.at[mid - s + 1, h], rs_l.at[s - 1, h], rsl_send.at[s - 1, h],
            rsl_recv.at[s - 1, h], left,
        )

    sent = []
    for h in range(2):

        def down_step(i, carry):
            for w in range(experts):
                part = jnp.dot(
                    act[w], wd_v[w, :, cols(i, h * half)], preferred_element_type=f32
                )
                xs[:, h, w * rows_e : (w + 1) * rows_e, cols(i)] = part.astype(bf16).reshape(
                    n, rows_e, STEP
                )
            return carry

        lax.fori_loop(0, steps, down_step, 0)
        for go in (back_right, back_left):
            if (go is back_right) == (h == 0):
                sent.append(go(1, h))
            else:
                sent.append(go(2, h))
            sent[-1].start()

    def add(slot, h, landed):
        def add_step(i, carry):
            c = cols(i)
            xs[slot, h, :, c] = (xs[slot, h, :, c].astype(f32) + landed[:, c].astype(f32)).astype(
                bf16
            )
            return carry

        lax.fori_loop(0, steps, add_step, 0)

    for s in range(2, mid + 1):
        for h in range(2):
            for go, first, slot, landing in (
                (back_right, 0, mid + s - 1, rs_r),
                (back_left, 1, mid - s + 1, rs_l),
            ):
                if s == 2 and h != first:
                    continue
                go(s - 1, h).wait_recv()
                add(slot, h, landing.at[s - 2, h])
                copy = go(s, h)
                copy.start()
                sent.append(copy)
    for h in range(2):
        back_right(mid, h).wait_recv()
        back_left(mid, h).wait_recv()

    def fold_step(i, carry):
        c = cols(i)
        total = None
        for h in range(2):
            mine = (
                xs[0, h, :, c].astype(f32)
                + rs_r[mid - 1, h, :, c].astype(f32)
                + rs_l[mid - 1, h, :, c].astype(f32)
            ).astype(bf16)
            part = jnp.dot(pmap[h], mine, preferred_element_type=f32)
            total = part if total is None else total + part
        total = total.astype(bf16).reshape(dp, 16, STEP)
        pack[:, :, c] = total
        ret[0, :, c] = total[0]
        return carry

    lax.fori_loop(0, steps, fold_step, 0)
    home = [
        remote(pack.at[k], ret.at[k], b_send.at[k], b_recv.at[k], across(dp - k))
        for k in range(1, dp)
    ]
    for copy in home:
        copy.start()
    for copy in home:
        copy.wait()

    def out_step(i, carry):
        rows = ret[:, :, cols(i)].reshape(dp * 16, STEP)
        for h in range(2):
            c = cols(i, h * half)
            picked = jnp.dot(bmap[h], rows, preferred_element_type=f32)
            out[:, c] = (hid[:, c].astype(f32) + wt[...] * picked).astype(bf16)
        return carry

    lax.fori_loop(0, steps, out_step, 0)
    for copy in sent:
        copy.wait_send()


def run_moe(dp, n, hidden_in, gain, amap, bmap, weight, qmap, pmap, w_gate, w_up, w_down):
    rows, width = hidden_in.shape
    experts, _, units = w_gate.shape
    half = width // 2
    mid = n // 2
    block = experts * dp * CAP
    bf16 = jnp.bfloat16
    dma = pltpu.SemaphoreType.DMA
    vmem = pl.BlockSpec(memory_space=pltpu.VMEM)
    hbm = pl.BlockSpec(memory_space=pl.ANY)
    return pl.pallas_call(
        functools.partial(moe_kernel, dp, n),
        out_shape=jax.ShapeDtypeStruct((rows, width), bf16),
        in_specs=[vmem] * 7 + [hbm] * 3,
        out_specs=vmem,
        scratch_shapes=[
            pltpu.VMEM((experts, width, units), bf16),
            pltpu.VMEM((experts, width, units), bf16),
            pltpu.VMEM((experts, units, width), bf16),
            pltpu.VMEM((dp, 16, half), bf16),
            pltpu.VMEM((dp, 16, half), bf16),
            pltpu.VMEM((dp, 16, half), bf16),
            pltpu.VMEM((n, 2, block, half), bf16),
            pltpu.VMEM((mid, 2, block, half), bf16),
            pltpu.VMEM((mid, 2, block, half), bf16),
            pltpu.VMEM((experts, n * block // experts, units), jnp.float32),
            pltpu.VMEM((experts, n * block // experts, units), jnp.float32),
            pltpu.VMEM((experts, n * block // experts, units), bf16),
            dma((3,)),
            dma((dp,)),
            dma((dp,)),
            dma((dp,)),
            dma((dp,)),
        ]
        + [dma((mid, 2))] * 8,
        compiler_params=pltpu.CompilerParams(
            collective_id=0, has_side_effects=True, vmem_limit_bytes=60 * 2**20
        ),
        cost_estimate=pl.CostEstimate(
            flops=6 * n * block * width * units,
            bytes_accessed=6 * experts * width * units,
            transcendentals=n * block * units,
        ),
        name="experts",
    )(hidden_in, gain, amap, bmap, weight, qmap, pmap, w_gate, w_up, w_down)


PAD = 640
TABLE = 256
SPAN = 896


def attend_kernel(q, pick, bias, fresh, pool, moved, out, pages, keys, qs, outs):
    f32 = jnp.float32
    bf16 = jnp.bfloat16
    groups = keys.shape[0]
    listed = MAXP * 8
    cached = listed * PAGE
    pairs = HEADS // 2
    extended = pool.shape[0] + moved.shape[0]

    @pl.when(pl.program_id(0) == 0)
    def _():
        pages[...] = jnp.zeros_like(pages)
        keys[:, cached:, :] = jnp.zeros((groups, SPAN - cached, PAD), bf16)
        keys[:, cached : cached + 16, :] = fresh[...]
        lane = lax.broadcasted_iota(jnp.int32, (extended, PAD), 1)

        def window(start):
            c = pl.ds(pl.multiple_of(start, 128), PAD)
            return jnp.concatenate([pool[:, c].astype(f32), moved[:, c].astype(f32)], axis=0)

        def split(i, carry):
            even = jnp.where(lane < KVW, window(i * (2 * KVW)), 0.0)
            odd = jnp.where(lane >= PAD - KVW, window(i * (2 * KVW) + 2 * KVW - PAD), 0.0)
            pages[2 * i, :extended, :] = even.astype(bf16)
            pages[2 * i + 1, :extended, :] = pltpu.roll(odd, KVW, 1).astype(bf16)
            return carry

        lax.fori_loop(0, PAGE // 2, split, 0)

        def gather(u, carry):
            rows = jnp.dot(pick[...], pages[u], preferred_element_type=f32).astype(bf16)
            keys[:, pl.ds(pl.multiple_of(u * listed, 16), listed), :] = rows.reshape(
                groups, listed, PAD
            )
            return carry

        lax.fori_loop(0, PAGE, gather, 0)

    for odd in range(2):

        def load(i, carry):
            start = pl.multiple_of(i * (2 * KVW) + odd * (2 * KVW - PAD), 128)
            x = q[:, pl.ds(start, PAD)].astype(f32)
            if odd:
                x = pltpu.roll(x, KVW, 1)
            at = pl.ds(pl.multiple_of(i * 8, 8), 8)
            qs[0, at, :] = x[:8]
            qs[1, at, :] = x[8:]
            return carry

        lax.fori_loop(0, pairs, load, 0, unroll=4)
        for sub in range(2):
            group = pl.program_id(0) * 2 + sub
            scores = lax.dot_general(
                qs[sub].astype(bf16),
                keys[group],
                (((1,), (1,)), ((), ())),
                preferred_element_type=f32,
            )
            scores = (
                scores.reshape(pairs, 8, SPAN) * softmax_scale
                + bias[sub * 8 : sub * 8 + 8, :][None]
            )
            top = jnp.max(scores, axis=2, keepdims=True)
            expo = jnp.exp(scores - top)
            total = jnp.sum(expo, axis=2, keepdims=True)
            probs = (expo * (1.0 / total)).reshape(pairs * 8, SPAN).astype(bf16)
            outs[sub] = jnp.dot(probs, keys[group, :, :LATENT], preferred_element_type=f32)

        def store(i, carry):
            at = pl.ds(pl.multiple_of(i * 8, 8), 8)
            rows = jnp.concatenate([outs[0, at, :], outs[1, at, :]], axis=0)
            start = pl.multiple_of(i * (2 * LATENT) + odd * LATENT, 128)
            out[:, pl.ds(start, LATENT)] = rows.astype(bf16)
            return carry

        lax.fori_loop(0, pairs, store, 0, unroll=4)


def run_attend(queries, page_table, kv_lengths, new_key, page_pool, moved):
    rows = queries.shape[0]
    groups = rows // 8
    listed = MAXP * 8
    bf16 = jnp.bfloat16
    pick = (page_table.reshape(rows * MAXP)[:, None] == jnp.arange(TABLE)[None, :]).astype(bf16)
    place = jnp.arange(SPAN)
    entry = place % listed
    owner = jnp.where(place < listed * PAGE, entry // MAXP, place - listed * PAGE)
    time = jnp.where(place < listed * PAGE, entry % MAXP * PAGE + place // listed, -1)
    mine = (jnp.arange(rows) % 8)[:, None] == owner[None, :]
    bias = jnp.where(mine & (time[None, :] < kv_lengths[:, None]), 0.0, -1e30)
    fresh = jnp.pad(new_key.reshape(groups, 8, KVW), ((0, 0), (0, 8), (0, PAD - KVW)))

    def whole(array):
        return pl.BlockSpec(array.shape, lambda i: (0,) * array.ndim)

    return pl.pallas_call(
        attend_kernel,
        grid=(rows // 16,),
        out_shape=jax.ShapeDtypeStruct((rows, HEADS * LATENT), bf16),
        in_specs=[
            pl.BlockSpec((16, HEADS * KVW), lambda i: (i, 0)),
            whole(pick),
            pl.BlockSpec((16, SPAN), lambda i: (i, 0)),
            whole(fresh),
            whole(page_pool),
            whole(moved),
        ],
        out_specs=pl.BlockSpec((16, HEADS * LATENT), lambda i: (i, 0)),
        scratch_shapes=[
            pltpu.VMEM((PAGE, TABLE, PAD), bf16),
            pltpu.VMEM((groups, SPAN, PAD), bf16),
            pltpu.VMEM((2, HEADS * 4, PAD), jnp.float32),
            pltpu.VMEM((2, HEADS * 4, LATENT), jnp.float32),
        ],
        compiler_params=pltpu.CompilerParams(vmem_limit_bytes=56 * 2**20),
        cost_estimate=pl.CostEstimate(
            flops=4 * rows * HEADS * SPAN * PAD,
            bytes_accessed=2 * rows * HEADS * (KVW + LATENT),
            transcendentals=rows * HEADS * SPAN,
        ),
        name="attend",
    )(queries, pick, bias, fresh, page_pool, moved)


def body(
    hidden_in,
    norm_gain,
    route_logits,
    expert_ids,
    w_gate,
    w_up,
    w_down,
    w_latent,
    kv_gain,
    queries,
    page_pool,
    page_table,
    kv_lengths,
    migration,
):
    dp_count = lax.axis_size("dp")
    local_experts = w_gate.shape[0]
    window = local_experts * dp_count
    flat_list = migration.reshape(dp_count * MCAP)
    outgoing = jnp.take(page_pool, flat_list, axis=0).reshape(dp_count, MCAP, page_pool.shape[1])
    incoming = lax.all_to_all(outgoing, "dp", split_axis=0, concat_axis=0, tiled=True)
    in_window = expert_ids < window
    has = jnp.any(in_window, axis=1)
    chosen = jnp.sum(jnp.where(in_window, expert_ids, 0), axis=1)
    sigma = jax.nn.sigmoid(route_logits)
    weight = (
        routed_scale * jnp.sum(jnp.where(in_window, sigma, 0.0), axis=1) / jnp.sum(sigma, axis=1)
    )
    onehot = ((chosen[:, None] == jnp.arange(window)[None, :]) & has[:, None]).astype(jnp.int32)
    rank = jnp.cumsum(onehot, axis=0) - onehot
    slot = jnp.sum(rank * onehot, axis=1)
    group = chosen // local_experts
    within = chosen % local_experts
    apart = (group - lax.axis_index("dp") + dp_count) % dp_count
    halves = jnp.arange(2)[:, None, None]
    target = apart * 16 + within * CAP + slot
    lines = jnp.arange(dp_count * 16)
    hit = (target[None, :, None] + 8 * halves == lines[None, None, :]) & has[None, :, None]
    back_map = hit.astype(jnp.bfloat16)
    send_map = jnp.swapaxes(back_map, 1, 2)
    block = local_experts * dp_count * CAP
    places = jnp.arange(block)
    own_expert = places // (dp_count * CAP)
    source = places // CAP % dp_count
    origin = source * 16 + own_expert * CAP + places % CAP
    sort_map = (origin[None, :, None] + 8 * halves == lines[None, None, :]).astype(jnp.bfloat16)
    hidden_out = run_moe(
        dp_count,
        lax.axis_size("expert"),
        hidden_in,
        norm_gain[None, :],
        send_map,
        back_map,
        jnp.where(has, weight, 0.0)[:, None],
        sort_map,
        jnp.swapaxes(sort_map, 1, 2),
        w_gate,
        w_up,
        w_down,
    )
    projected = jnp.dot(
        hidden_out,
        lax.all_gather(w_latent, ("dp", "expert"), axis=0, tiled=True),
        preferred_element_type=jnp.float32,
    )
    latent = rms_rows(projected[:, :LATENT], kv_gain)
    rotary = rotate_keys(projected[:, LATENT:], kv_lengths.astype(jnp.float32))
    new_key = jnp.concatenate([latent, rotary], axis=1).astype(jnp.bfloat16)
    moved = incoming.reshape(dp_count * MCAP, page_pool.shape[1])
    attended = run_attend(queries, page_table, kv_lengths, new_key, page_pool, moved)
    return (hidden_out, attended)


def solution(mesh):
    return jax.shard_map(
        body,
        mesh=mesh,
        in_specs=(
            P(("dp", "expert"), None),
            P(),
            P(("dp", "expert"), None),
            P(("dp", "expert"), None),
            P("dp", None, "expert"),
            P("dp", None, "expert"),
            P("dp", "expert", None),
            P(("dp", "expert"), None),
            P(),
            P(("dp", "expert"), None),
            P(("dp", "expert"), None),
            P(("dp", "expert"), None),
            P(("dp", "expert")),
            P("dp", "expert", None, None),
        ),
        out_specs=(P(("dp", "expert"), None), P(("dp", "expert"), None)),
        check_vma=False,
    )
```
